128 devices in a mesh: ctx: 16 (over y_hi, z, core), dp: 8 (over x, y_lo).
Axes of the slice: x: 4, y: 4 (y_hi: 2, y_lo: 2; y = y_hi * 2 + y_lo), z: 4, core: 2. Of those that a mesh axis runs over, the one named last changes fastest.
Arguments:
- queries: bfloat16 [16384, 4096], P(('dp', 'ctx')), parts along dimension 0, may hold values from -144 to 144
- keys: bfloat16 [16384, 4096], P(('dp', 'ctx')), parts along dimension 0, may hold values from -6.1 to 6.1
- values: bfloat16 [16384, 4096], P(('dp', 'ctx')), parts along dimension 0, may hold values from -6 to 6
- query_tangent: bfloat16 [16384, 4096], P(('dp', 'ctx')), parts along dimension 0, may hold values from -6 to 6
- key_tangent: bfloat16 [16384, 4096], P(('dp', 'ctx')), parts along dimension 0, may hold values from -6 to 6
- value_tangent: bfloat16 [16384, 4096], P(('dp', 'ctx')), parts along dimension 0, may hold values from -6 to 6
Outputs:
- attended: bfloat16 [16384, 4096], P(('dp', 'ctx')), parts along dimension 0
- attended_tangent: bfloat16 [16384, 4096], P(('dp', 'ctx')), parts along dimension 0
The draws below stay inside these ranges and needn't reach their ends.
There are 8 independent parts, one for each index of `dp`. The reference program is written for one: setup_inputs(seed, part) draws one part's arguments, and reference() takes and returns one part's arrays. A program takes and returns all parts, laid end to end along the dimension named above; each array names one. Nothing has to cross between parts.
All inputs are finite; a program needn't handle non-finite values.
Results may differ from the reference program's by a relative error of at most 0.005.
Values may be sent and summed in bfloat16 or wider, within the bound.
A program may use at most 64 MiB of HBM per device.

```python
import jax
import jax.numpy as jnp
from jax import lax

HEADS = 32
HEAD_DIM = 128
TOKENS = 2048


def key_rows(key):
    return jnp.clip(jax.random.normal(key, (TOKENS, HEADS * HEAD_DIM), jnp.float32), -6.0, 6.0)


def draw_keys(key, part):
    key_base = key_rows(key)
    return key_base.astype(jnp.bfloat16)


def draw_queries(key, part):
    key = jax.random.fold_in(key, 23)
    fresh = jax.random.normal(key, (TOKENS, HEADS * HEAD_DIM), jnp.float32)
    result = jnp.clip(fresh * 2.5, -15.0, 15.0)
    return result.astype(jnp.bfloat16)


def shard_levels(rng, shape, cuts, low, top_value):
    def one(position, blocks):
        heights = jax.random.uniform(jax.random.fold_in(jax.random.fold_in(rng, 6), position), (blocks,), jnp.float32, low / len(cuts), top_value / len(cuts))
        return jnp.repeat(jnp.exp(heights), shape[position] // blocks).reshape((-1,) + (1,) * (len(shape) - position - 1))

    loudness = one(*cuts[0])
    for cut in cuts[1:]:
        loudness = loudness * one(*cut)
    return loudness


def scatter_about(key, extent, width, limit, split=(), held_as=jnp.bfloat16):
    loudness = shard_levels(key, extent, split, -0.22, 0.18) if split else 1.0
    values = jax.random.normal(key, extent, jnp.float32) * width * loudness
    return jnp.minimum(jnp.maximum(values, -limit), limit).astype(held_as)


def setup_inputs(seed: int = 0, part: int = 0) -> dict:
    key_list = jax.random.split(jax.random.key(seed), 7)
    part_splits = jax.random.split(jax.random.fold_in(key_list[6], part), 7)
    return {
        "queries": draw_queries(jax.random.fold_in(jax.random.fold_in(key_list[6], part), 71), part),
        "keys": draw_keys(jax.random.fold_in(jax.random.fold_in(key_list[6], part), 71), part),
        "values": scatter_about(part_splits[2], (TOKENS, HEADS * HEAD_DIM), 1.0, 6.0, ((0, 16),)),
        "query_tangent": scatter_about(part_splits[3], (TOKENS, HEADS * HEAD_DIM), 1.0, 6.0, ((0, 16),)),
        "key_tangent": scatter_about(part_splits[4], (TOKENS, HEADS * HEAD_DIM), 1.0, 6.0, ((0, 16),)),
        "value_tangent": scatter_about(part_splits[5], (TOKENS, HEADS * HEAD_DIM), 1.0, 6.0, ((0, 16),)),
    }


def by_head(array):
    return array.reshape(TOKENS, HEADS, HEAD_DIM).transpose(1, 0, 2)


def single_head(operands):
    query, key_head, value_head, query_delta, key_delta, value_delta = operands
    factor = HEAD_DIM ** -0.5
    scores = jnp.dot(query, key_head.T, preferred_element_type=jnp.float32) * factor
    shifted = jnp.exp(scores - jnp.max(scores, axis=-1, keepdims=True))
    weights = shifted / jnp.sum(shifted, axis=-1, keepdims=True)
    rounded = weights.astype(jnp.bfloat16)
    output = jnp.dot(rounded, value_head, preferred_element_type=jnp.float32)
    delta = (jnp.dot(query_delta, key_head.T, preferred_element_type=jnp.float32)
             + jnp.dot(query, key_delta.T, preferred_element_type=jnp.float32)) * factor
    centre = jnp.sum(weights * delta, axis=-1, keepdims=True)
    weight_delta = (weights * (delta - centre)).astype(jnp.bfloat16)
    output_delta = (jnp.dot(weight_delta, value_head, preferred_element_type=jnp.float32)
                    + jnp.dot(rounded, value_delta, preferred_element_type=jnp.float32))
    return output.astype(jnp.bfloat16), output_delta.astype(jnp.bfloat16)


def reference(queries, keys, values, query_tangent, key_tangent, value_tangent):
    operands = (by_head(queries), by_head(keys), by_head(values),
                by_head(query_tangent), by_head(key_tangent), by_head(value_tangent))
    output, output_delta = lax.map(single_head, operands)
    attended = output.transpose(1, 0, 2).reshape(TOKENS, HEADS * HEAD_DIM)
    attended_tangent = output_delta.transpose(1, 0, 2).reshape(TOKENS, HEADS * HEAD_DIM)
    return attended, attended_tangent
```

```python
import functools

import jax
import jax.numpy as jnp
from jax import lax
from jax.experimental import pallas as pl
from jax.experimental.pallas import tpu as pltpu
from jax.sharding import PartitionSpec as P

HEAD_DIM = 128
MESH = pl.DeviceIdType.MESH
Z = 4
CORES = 2
F32 = jnp.float32
BF16 = jnp.bfloat16


def attend(query, query_delta, key, key_delta, value, value_delta):
    factor = HEAD_DIM**-0.5
    across = (((1,), (1,)), ((), ()))
    scores = lax.dot_general(query, key, across, preferred_element_type=F32)
    delta = lax.dot_general(
        jnp.concatenate([query_delta, query], axis=1),
        jnp.concatenate([key, key_delta], axis=1),
        across,
        preferred_element_type=F32,
    )
    top = jnp.max(scores, axis=1, keepdims=True)
    shifted = jnp.exp((scores - top) * factor)
    scale = 1.0 / jnp.sum(shifted, axis=1, keepdims=True)
    centre = jnp.sum(shifted * delta, axis=1, keepdims=True) * scale
    weights = shifted * scale
    weight_delta = (weights * ((delta - centre) * factor)).astype(BF16)
    both = jnp.dot(
        weights.astype(BF16),
        jnp.concatenate([value, value_delta], axis=1),
        preferred_element_type=F32,
    )
    moved = jnp.dot(weight_delta, value, preferred_element_type=F32)
    return both[:, :HEAD_DIM].astype(BF16), (moved + both[:, HEAD_DIM:]).astype(BF16)


def kernel(
    q_in, k_in, v_in, dq_in, dk_in, dv_in,
    out, out_delta,
    kv, qs, res,
    kv_send, kv_recv, q_send, q_recv, o_send, o_recv,
):
    me = lax.axis_index("ctx")
    rows, wide = q_in.shape[0], kv.shape[2]
    n = lax.axis_size("ctx")
    chips = n // CORES
    y_count = chips // Z
    heads = wide // HEAD_DIM
    pair = CORES * rows
    core = lax.rem(me, CORES)
    z = lax.rem(me // CORES, Z)
    y = me // (CORES * Z)

    def chip_at(step, sign):
        dy, dz = step // Z, lax.rem(step, Z)
        there_y = lax.rem(y + sign * dy + y_count, y_count)
        there_z = lax.rem(z + sign * dz + Z, Z)
        return there_y * Z + there_z

    def each_partner(step, act):
        chip = chip_at(step, 1)
        for turn in range(CORES):
            act(chip * CORES + lax.rem(core + turn, CORES))

    def other_core(act):
        for turn in range(1, CORES):
            act(me - core + lax.rem(core + turn, CORES))

    barrier = pltpu.get_barrier_semaphore()

    def greet(device):
        pl.semaphore_signal(barrier, inc=1, device_id={"ctx": device}, device_id_type=MESH)

    other_core(greet)

    def greet_chip(step, carry):
        each_partner(step, greet)
        return carry

    lax.fori_loop(1, chips, greet_chip, 0)
    pl.semaphore_wait(barrier, n - 1)

    mine = pl.ds(pl.multiple_of(me * rows, rows), rows)

    def columns(device):
        return pl.ds(pl.multiple_of(device * wide, wide), wide)

    def send(src, dst, send_sem, recv_sem, device):
        pltpu.make_async_remote_copy(
            src_ref=src, dst_ref=dst, send_sem=send_sem, recv_sem=recv_sem,
            device_id={"ctx": device}, device_id_type=MESH,
        ).start()

    def send_kv(device):
        for i, array in enumerate((k_in, dk_in, v_in, dv_in)):
            send(array.at[:, columns(device)], kv.at[i, mine, :], kv_send, kv_recv, device)

    def send_q(device):
        for i, array in enumerate((q_in, dq_in)):
            send(array.at[:, columns(device)], qs.at[i, mine, :], q_send, q_recv.at[me // CORES], device)

    for i, array in enumerate((k_in, dk_in, v_in, dv_in)):
        pltpu.make_async_copy(array.at[:, columns(me)], kv.at[i, mine, :], kv_recv).start()
    for i, array in enumerate((q_in, dq_in)):
        pltpu.make_async_copy(array.at[:, columns(me)], qs.at[i, mine, :], q_recv.at[me // CORES]).start()

    def kv_chip(i, carry):
        each_partner(chips - i, send_kv)
        return carry

    def q_chip(i, carry):
        each_partner(chips - i, send_q)
        return carry

    other_core(send_kv)
    lax.fori_loop(1, chips, kv_chip, 0)
    other_core(send_q)
    lax.fori_loop(1, chips, q_chip, 0)

    def drain(ref, sem):
        pltpu.make_async_copy(ref, ref, sem).wait()

    drain(kv, kv_recv)

    def finish(chip):
        block = pl.ds(pl.multiple_of(chip * pair, pair), pair)
        drain(qs.at[:, block, :], q_recv.at[chip])
        for head in range(heads):
            lanes = pl.ds(head * HEAD_DIM, HEAD_DIM)
            primal, tangent = attend(
                qs[0, block, lanes], qs[1, block, lanes],
                kv[0, :, lanes], kv[1, :, lanes], kv[2, :, lanes], kv[3, :, lanes],
            )
            res[0, block, lanes] = primal
            res[1, block, lanes] = tangent

    def send_res(device):
        owned = pl.ds(pl.multiple_of(device * rows, rows), rows)
        for i, array in enumerate((out, out_delta)):
            send(res.at[i, owned, :], array.at[:, columns(me)], o_send, o_recv.at[i], device)

    finish(me // CORES)
    for i, array in enumerate((out, out_delta)):
        pltpu.make_async_copy(res.at[i, mine, :], array.at[:, columns(me)], o_recv.at[i]).start()
    other_core(send_res)

    def step_chip(i, carry):
        chip = chip_at(chips - i, -1)
        finish(chip)
        for turn in range(CORES):
            send_res(chip * CORES + lax.rem(core + turn, CORES))
        return carry

    lax.fori_loop(1, chips, step_chip, 0)

    others = pl.ds(0, (n - 1) * rows)
    drain(kv.at[:, others, :], kv_send)
    drain(qs.at[:, others, :], q_send)
    drain(res.at[:, others, :], o_send)
    drain(out, o_recv.at[0])
    drain(out_delta, o_recv.at[1])


def body(*arrays):
    rows, width = arrays[0].shape
    n = lax.axis_size("ctx")
    tokens, wide = rows * n, width // n
    heads = width // HEAD_DIM
    anywhere = pl.BlockSpec(memory_space=pl.ANY)
    dma = pltpu.SemaphoreType.DMA
    products = 6 * 2 * tokens * tokens * HEAD_DIM * heads // n
    return pl.pallas_call(
        kernel,
        out_shape=(jax.ShapeDtypeStruct((rows, width), BF16),) * 2,
        in_specs=[anywhere] * 6,
        out_specs=(anywhere,) * 2,
        scratch_shapes=[
            pltpu.VMEM((4, tokens, wide), BF16),
            pltpu.VMEM((2, tokens, wide), BF16),
            pltpu.VMEM((2, tokens, wide), BF16),
            dma, dma, dma, dma((n // CORES,)), dma, dma((2,)),
        ],
        compiler_params=pltpu.CompilerParams(
            collective_id=0, has_side_effects=True, vmem_limit_bytes=60 << 20
        ),
        cost_estimate=pl.CostEstimate(
            flops=products, bytes_accessed=8 * rows * width * 2, transcendentals=tokens * tokens * heads // n
        ),
        name="attend_exchange",
    )(*arrays)


def solution(mesh):
    spec = P(("dp", "ctx"), None)
    return jax.shard_map(body, mesh=mesh, in_specs=(spec,) * 6, out_specs=(spec,) * 2, check_vma=False)
```

```python
import functools

import jax
import jax.numpy as jnp
from jax import lax
from jax.experimental import pallas as pl
from jax.experimental.pallas import tpu as pltpu
from jax.sharding import PartitionSpec as P

HEAD_DIM = 128
MESH = pl.DeviceIdType.MESH
Z = 4
CORES = 2
F32 = jnp.float32
BF16 = jnp.bfloat16


def attend(query, query_delta, key, key_delta, value, value_delta):
    factor = HEAD_DIM**-0.5
    across = (((1,), (1,)), ((), ()))
    scores = lax.dot_general(query, key, across, preferred_element_type=F32)
    delta = lax.dot_general(
        jnp.concatenate([query_delta, query], axis=1),
        jnp.concatenate([key, key_delta], axis=1),
        across,
        preferred_element_type=F32,
    )
    top = jnp.max(scores, axis=1, keepdims=True)
    shifted = jnp.exp((scores - top) * factor)
    scale = 1.0 / jnp.sum(shifted, axis=1, keepdims=True)
    centre = jnp.sum(shifted * delta, axis=1, keepdims=True) * scale
    weights = shifted * scale
    weight_delta = (weights * ((delta - centre) * factor)).astype(BF16)
    both = jnp.dot(
        weights.astype(BF16),
        jnp.concatenate([value, value_delta], axis=1),
        preferred_element_type=F32,
    )
    moved = jnp.dot(weight_delta, value, preferred_element_type=F32)
    return both[:, :HEAD_DIM].astype(BF16), (moved + both[:, HEAD_DIM:]).astype(BF16)


def kernel(
    q_in, k_in, v_in, dq_in, dk_in, dv_in,
    out, out_delta,
    kv, qs, res,
    kv_send, kv_recv, q_send, q_recv, o_send, o_recv,
):
    me = lax.axis_index("ctx")
    rows = q_in.shape[0]
    n = lax.axis_size("ctx")
    chips = n // CORES
    y_count = chips // Z
    heads = kv.shape[0]
    wide = heads * HEAD_DIM
    pair = CORES * rows
    core = lax.rem(me, CORES)
    z = lax.rem(me // CORES, Z)
    y = me // (CORES * Z)

    def chip_at(step, sign):
        dy, dz = step // Z, lax.rem(step, Z)
        there_y = lax.rem(y + sign * dy + y_count, y_count)
        there_z = lax.rem(z + sign * dz + Z, Z)
        return there_y * Z + there_z

    def each_partner(step, act):
        chip = chip_at(step, 1)
        for turn in range(CORES):
            act(chip * CORES + lax.rem(core + turn, CORES))

    def other_core(act):
        for turn in range(1, CORES):
            act(me - core + lax.rem(core + turn, CORES))

    barrier = pltpu.get_barrier_semaphore()

    def greet(device):
        pl.semaphore_signal(barrier, inc=1, device_id={"ctx": device}, device_id_type=MESH)

    other_core(greet)

    def greet_chip(step, carry):
        each_partner(step, greet)
        return carry

    lax.fori_loop(1, chips, greet_chip, 0)
    pl.semaphore_wait(barrier, n - 1)

    mine = pl.ds(pl.multiple_of(me * rows, rows), rows)

    def columns(device, head):
        return pl.ds(pl.multiple_of(device * wide + head * HEAD_DIM, HEAD_DIM), HEAD_DIM)

    def send(src, dst, send_sem, recv_sem, device):
        pltpu.make_async_remote_copy(
            src_ref=src, dst_ref=dst, send_sem=send_sem, recv_sem=recv_sem,
            device_id={"ctx": device}, device_id_type=MESH,
        ).start()

    def send_kv(head, device):
        for i, array in enumerate((k_in, dk_in, v_in, dv_in)):
            send(
                array.at[:, columns(device, head)], kv.at[head, i, mine, :],
                kv_send.at[head], kv_recv.at[head], device,
            )

    def send_q(head, device):
        for i, array in enumerate((q_in, dq_in)):
            send(
                array.at[:, columns(device, head)], qs.at[head, i, mine, :],
                q_send.at[head], q_recv.at[head, me // CORES], device,
            )

    def start_head(head, carry):
        for i, array in enumerate((k_in, dk_in, v_in, dv_in)):
            pltpu.make_async_copy(
                array.at[:, columns(me, head)], kv.at[head, i, mine, :], kv_recv.at[head]
            ).start()
        for i, array in enumerate((q_in, dq_in)):
            pltpu.make_async_copy(
                array.at[:, columns(me, head)], qs.at[head, i, mine, :], q_recv.at[head, me // CORES]
            ).start()
        for part in (send_kv, send_q):
            part = functools.partial(part, head)

            def to_chip(i, carry, part=part):
                each_partner(chips - i, part)
                return carry

            other_core(part)
            lax.fori_loop(1, chips, to_chip, 0)
        return carry

    lax.fori_loop(0, heads, start_head, 0)

    def drain(ref, sem):
        pltpu.make_async_copy(ref, ref, sem).wait()

    def send_res(head, device):
        owned = pl.ds(pl.multiple_of(device * rows, rows), rows)
        for i, array in enumerate((out, out_delta)):
            send(res.at[head, i, owned, :], array.at[:, columns(me, head)], o_send, o_recv.at[i], device)

    def step_chip(i, carry):
        head, step = i // chips, lax.rem(i, chips)
        chip = chip_at(lax.rem(chips - step, chips), -1)

        @pl.when(step == 0)
        def _():
            drain(kv.at[head], kv_recv.at[head])

        block = pl.ds(pl.multiple_of(chip * pair, pair), pair)
        drain(qs.at[head, :, block, :], q_recv.at[head, chip])
        primal, tangent = attend(
            qs[head, 0, block, :], qs[head, 1, block, :],
            kv[head, 0], kv[head, 1], kv[head, 2], kv[head, 3],
        )
        res[head, 0, block, :] = primal
        res[head, 1, block, :] = tangent

        @pl.when(step == 0)
        def _():
            for j, array in enumerate((out, out_delta)):
                pltpu.make_async_copy(
                    res.at[head, j, mine, :], array.at[:, columns(me, head)], o_recv.at[j]
                ).start()
            other_core(functools.partial(send_res, head))

        @pl.when(step != 0)
        def _():
            for turn in range(CORES):
                send_res(head, chip * CORES + lax.rem(core + turn, CORES))

        return carry

    lax.fori_loop(0, heads * chips, step_chip, 0)

    others = pl.ds(0, (n - 1) * rows)
    for head in range(heads):
        drain(kv.at[head, :, others, :], kv_send.at[head])
        drain(qs.at[head, :, others, :], q_send.at[head])
    drain(res.at[:, :, others, :], o_send)
    drain(out, o_recv.at[0])
    drain(out_delta, o_recv.at[1])


def body(*arrays):
    rows, width = arrays[0].shape
    n = lax.axis_size("ctx")
    tokens = rows * n
    heads = width // HEAD_DIM // n
    anywhere = pl.BlockSpec(memory_space=pl.ANY)
    dma = pltpu.SemaphoreType.DMA
    products = 6 * 2 * tokens * tokens * HEAD_DIM * heads
    return pl.pallas_call(
        kernel,
        out_shape=(jax.ShapeDtypeStruct((rows, width), BF16),) * 2,
        in_specs=[anywhere] * 6,
        out_specs=(anywhere,) * 2,
        scratch_shapes=[
            pltpu.VMEM((heads, 4, tokens, HEAD_DIM), BF16),
            pltpu.VMEM((heads, 2, tokens, HEAD_DIM), BF16),
            pltpu.VMEM((heads, 2, tokens, HEAD_DIM), BF16),
            dma((heads,)), dma((heads,)), dma((heads,)), dma((heads, n // CORES)), dma, dma((2,)),
        ],
        compiler_params=pltpu.CompilerParams(
            collective_id=0, has_side_effects=True, vmem_limit_bytes=60 << 20
        ),
        cost_estimate=pl.CostEstimate(
            flops=products, bytes_accessed=8 * rows * width * 2, transcendentals=tokens * tokens * heads
        ),
        name="attend_exchange",
    )(*arrays)


def solution(mesh):
    spec = P(("dp", "ctx"), None)
    return jax.shard_map(body, mesh=mesh, in_specs=(spec,) * 6, out_specs=(spec,) * 2, check_vma=False)
```

```python
import functools

import jax
import jax.numpy as jnp
from jax import lax
from jax.experimental import pallas as pl
from jax.experimental.pallas import tpu as pltpu
from jax.sharding import PartitionSpec as P

HEAD_DIM = 128
MESH = pl.DeviceIdType.MESH
Z = 4
CORES = 2
F32 = jnp.float32
BF16 = jnp.bfloat16


def attend(query, query_delta, key, key_delta, value, value_delta):
    factor = HEAD_DIM**-0.5
    across = (((1,), (1,)), ((), ()))
    scores = lax.dot_general(query, key, across, preferred_element_type=F32)
    delta = lax.dot_general(
        jnp.concatenate([query_delta, query], axis=1),
        jnp.concatenate([key, key_delta], axis=1),
        across,
        preferred_element_type=F32,
    )
    top = jnp.max(scores, axis=1, keepdims=True)
    shifted = jnp.exp((scores - top) * factor)
    scale = 1.0 / jnp.sum(shifted, axis=1, keepdims=True)
    centre = jnp.sum(shifted * delta, axis=1, keepdims=True) * scale
    weights = shifted * scale
    weight_delta = (weights * ((delta - centre) * factor)).astype(BF16)
    both = jnp.dot(
        weights.astype(BF16),
        jnp.concatenate([value, value_delta], axis=1),
        preferred_element_type=F32,
    )
    moved = jnp.dot(weight_delta, value, preferred_element_type=F32)
    return both[:, :HEAD_DIM].astype(BF16), (moved + both[:, HEAD_DIM:]).astype(BF16)


def kernel(
    q_in, k_in, v_in, dq_in, dk_in, dv_in,
    out, out_delta,
    kv, qs, res,
    kv_send, kv_recv, q_send, q_recv, o_send, o_recv,
):
    me = lax.axis_index("ctx")
    rows = q_in.shape[0]
    n = lax.axis_size("ctx")
    chips = n // CORES
    y_count = chips // Z
    heads = kv.shape[0]
    wide = heads * HEAD_DIM
    pair = CORES * rows
    core = lax.rem(me, CORES)
    z = lax.rem(me // CORES, Z)
    y = me // (CORES * Z)

    def chip_at(step, sign, way):
        dy, dz = step // Z, lax.rem(step, Z)
        there_y = lax.rem(y + sign * dy + y_count, y_count)
        there_z = lax.rem(z + sign * way * dz + Z, Z)
        return there_y * Z + there_z

    def each_partner(step, act):
        chip = chip_at(step, 1, 1 - 2 * core)
        for turn in range(CORES):
            act(chip * CORES + lax.rem(core + turn, CORES))

    def other_core(act):
        for turn in range(1, CORES):
            act(me - core + lax.rem(core + turn, CORES))

    barrier = pltpu.get_barrier_semaphore()

    def greet(device):
        pl.semaphore_signal(barrier, inc=1, device_id={"ctx": device}, device_id_type=MESH)

    other_core(greet)

    def greet_chip(step, carry):
        each_partner(step, greet)
        return carry

    lax.fori_loop(1, chips, greet_chip, 0)
    pl.semaphore_wait(barrier, n - 1)

    mine = pl.ds(pl.multiple_of(me * rows, rows), rows)

    def columns(device, head):
        return pl.ds(pl.multiple_of(device * wide + head * HEAD_DIM, HEAD_DIM), HEAD_DIM)

    def send(src, dst, send_sem, recv_sem, device):
        pltpu.make_async_remote_copy(
            src_ref=src, dst_ref=dst, send_sem=send_sem, recv_sem=recv_sem,
            device_id={"ctx": device}, device_id_type=MESH,
        ).start()

    def start_head(head, carry):
        groups = (
            (kv, (k_in, dk_in, v_in, dv_in), kv_send.at[head], kv_recv.at[head]),
            (qs, (q_in, dq_in), q_send.at[head], q_recv.at[head, me // CORES]),
        )
        for buffer, arrays, send_sem, recv_sem in groups:
            for i, array in enumerate(arrays):
                there = buffer.at[head, i, mine, :]
                pltpu.make_async_copy(array.at[:, columns(me, head)], there, recv_sem).start()

                def to_device(device, array=array, there=there, send_sem=send_sem, recv_sem=recv_sem):
                    send(array.at[:, columns(device, head)], there, send_sem, recv_sem, device)

                def to_chip(i, carry, act=to_device):
                    each_partner(chips - i, act)
                    return carry

                other_core(to_device)
                lax.fori_loop(1, chips, to_chip, 0)
        return carry

    lax.fori_loop(0, heads, start_head, 0)

    def drain(ref, sem):
        pltpu.make_async_copy(ref, ref, sem).wait()

    def send_res(head, device):
        owned = pl.ds(pl.multiple_of(device * rows, rows), rows)
        for i, array in enumerate((out, out_delta)):
            send(res.at[head, i, owned, :], array.at[:, columns(me, head)], o_send, o_recv.at[i], device)

    def step_chip(i, carry):
        head, step = i // chips, lax.rem(i, chips)
        chip = chip_at(lax.rem(chips - step, chips), -1, 1)

        @pl.when(step == 0)
        def _():
            drain(kv.at[head], kv_recv.at[head])

        block = pl.ds(pl.multiple_of(chip * pair, pair), pair)
        drain(qs.at[head, :, block, :], q_recv.at[head, chip])
        primal, tangent = attend(
            qs[head, 0, block, :], qs[head, 1, block, :],
            kv[head, 0], kv[head, 1], kv[head, 2], kv[head, 3],
        )
        res[head, 0, block, :] = primal
        res[head, 1, block, :] = tangent

        @pl.when(step == 0)
        def _():
            for j, array in enumerate((out, out_delta)):
                pltpu.make_async_copy(
                    res.at[head, j, mine, :], array.at[:, columns(me, head)], o_recv.at[j]
                ).start()
            other_core(functools.partial(send_res, head))

        @pl.when(step != 0)
        def _():
            for turn in range(CORES):
                send_res(head, chip * CORES + lax.rem(core + turn, CORES))

        return carry

    lax.fori_loop(0, heads * chips, step_chip, 0)

    others = pl.ds(0, (n - 1) * rows)
    for head in range(heads):
        drain(kv.at[head, :, others, :], kv_send.at[head])
        drain(qs.at[head, :, others, :], q_send.at[head])
    drain(res.at[:, :, others, :], o_send)
    drain(out, o_recv.at[0])
    drain(out_delta, o_recv.at[1])


def settle_kernel(a, b, out_a, out_b, sems):
    copies = [pltpu.make_async_copy(a, out_a, sems.at[0]), pltpu.make_async_copy(b, out_b, sems.at[1])]
    for copy in copies:
        copy.start()
    for copy in copies:
        copy.wait()


def settle(a, b, space):
    anywhere = pl.BlockSpec(memory_space=pl.ANY)
    return pl.pallas_call(
        settle_kernel,
        out_shape=(jax.ShapeDtypeStruct(a.shape, a.dtype),) * 2,
        in_specs=[space] * 2,
        out_specs=(anywhere,) * 2,
        scratch_shapes=[pltpu.SemaphoreType.DMA((2,))],
        name="settle",
    )(a, b)


def body(*arrays):
    rows, width = arrays[0].shape
    n = lax.axis_size("ctx")
    tokens = rows * n
    heads = width // HEAD_DIM // n
    anywhere = pl.BlockSpec(memory_space=pl.ANY)
    dma = pltpu.SemaphoreType.DMA
    products = 6 * 2 * tokens * tokens * HEAD_DIM * heads
    result = pl.pallas_call(
        kernel,
        out_shape=(pltpu.VMEM((rows, width), BF16),) * 2,
        in_specs=[anywhere] * 6,
        out_specs=(pl.BlockSpec(memory_space=pltpu.VMEM),) * 2,
        scratch_shapes=[
            pltpu.VMEM((heads, 4, tokens, HEAD_DIM), BF16),
            pltpu.VMEM((heads, 2, tokens, HEAD_DIM), BF16),
            pltpu.VMEM((heads, 2, tokens, HEAD_DIM), BF16),
            dma((heads,)), dma((heads,)), dma((heads,)), dma((heads, n // CORES)), dma, dma((2,)),
        ],
        compiler_params=pltpu.CompilerParams(
            collective_id=0, has_side_effects=True, vmem_limit_bytes=60 << 20
        ),
        cost_estimate=pl.CostEstimate(
            flops=products, bytes_accessed=8 * rows * width * 2, transcendentals=tokens * tokens * heads
        ),
        name="attend_exchange",
    )(*arrays)
    result = [pltpu.with_memory_space_constraint(r, pltpu.VMEM) for r in result]
    return settle(*result, pl.BlockSpec(memory_space=pltpu.VMEM))


def solution(mesh):
    spec = P(("dp", "ctx"), None)
    return jax.shard_map(body, mesh=mesh, in_specs=(spec,) * 6, out_specs=(spec,) * 2, check_vma=False)
```

```python
import functools
import math

import jax
import jax.numpy as jnp
from jax import lax
from jax.experimental import pallas as pl
from jax.experimental.pallas import tpu as pltpu
from jax.sharding import PartitionSpec as P

HEAD_DIM = 128
LOG2_E = math.log2(math.e)
MESH = pl.DeviceIdType.MESH
Z = 4
CORES = 2
F32 = jnp.float32
BF16 = jnp.bfloat16


def attend(queries, keys, values):
    factor = HEAD_DIM**-0.5
    across = (((1,), (1,)), ((), ()))
    scores = lax.dot_general(
        queries[:, HEAD_DIM:], keys[:, :HEAD_DIM], across, preferred_element_type=F32
    )
    delta = lax.dot_general(queries, keys, across, preferred_element_type=F32)
    top = jnp.max(scores, axis=1, keepdims=True)
    shifted = jnp.exp2((scores - top) * (factor * LOG2_E))
    scale = 1.0 / jnp.sum(shifted, axis=1, keepdims=True)
    centre = jnp.sum(shifted * delta, axis=1, keepdims=True) * scale
    weights = shifted * scale
    weight_delta = (weights * ((delta - centre) * factor)).astype(BF16)
    both = jnp.dot(weights.astype(BF16), values, preferred_element_type=F32)
    moved = jnp.dot(weight_delta, values[:, :HEAD_DIM], preferred_element_type=F32)
    return both[:, :HEAD_DIM].astype(BF16), (moved + both[:, HEAD_DIM:]).astype(BF16)


def kernel(
    q_in, k_in, v_in, dq_in, dk_in, dv_in,
    out, out_delta,
    kv, qs, res,
    kv_send, kv_recv, q_send, q_recv, o_send, o_recv,
):
    me = lax.axis_index("ctx")
    rows = q_in.shape[0]
    n = lax.axis_size("ctx")
    chips = n // CORES
    y_count = chips // Z
    heads = res.shape[0]
    wide = heads * HEAD_DIM
    pair = CORES * rows
    core = lax.rem(me, CORES)
    z = lax.rem(me // CORES, Z)
    y = me // (CORES * Z)

    def chip_at(step, sign, way):
        dy, dz = step // Z, lax.rem(step, Z)
        there_y = lax.rem(y + sign * dy + y_count, y_count)
        there_z = lax.rem(z + sign * way * dz + Z, Z)
        return there_y * Z + there_z

    def each_partner(step, act):
        chip = chip_at(step, 1, 1 - 2 * core)
        for turn in range(CORES):
            act(chip * CORES + lax.rem(core + turn, CORES))

    def other_core(act):
        for turn in range(1, CORES):
            act(me - core + lax.rem(core + turn, CORES))

    barrier = pltpu.get_barrier_semaphore()

    def greet(device):
        pl.semaphore_signal(barrier, inc=1, device_id={"ctx": device}, device_id_type=MESH)

    for step in range(chips - 1, 0, -1):
        each_partner(step, greet)
    other_core(greet)
    pl.semaphore_wait(barrier, n - 1)

    mine = pl.ds(pl.multiple_of(me * rows, rows), rows)

    def columns(device, head):
        return pl.ds(pl.multiple_of(device * wide + head * HEAD_DIM, HEAD_DIM), HEAD_DIM)

    def send(src, dst, send_sem, recv_sem, device):
        pltpu.make_async_remote_copy(
            src_ref=src, dst_ref=dst, send_sem=send_sem, recv_sem=recv_sem,
            device_id={"ctx": device}, device_id_type=MESH,
        ).start()

    def start_head(head, carry):
        groups = (
            ((k_in, dk_in, v_in, dv_in), (kv.at[head, 0], kv.at[head, 1]), kv_send.at[head], kv_recv.at[head]),
            ((dq_in, q_in), (qs.at[head],), q_send.at[head], q_recv.at[head, me // CORES]),
        )
        for arrays, pairs, send_sem, recv_sem in groups:
            for i, array in enumerate(arrays):
                there = pairs[i // 2].at[mine, pl.ds(i % 2 * HEAD_DIM, HEAD_DIM)]
                pltpu.make_async_copy(array.at[:, columns(me, head)], there, recv_sem).start()

                def to_device(device, array=array, there=there, send_sem=send_sem, recv_sem=recv_sem):
                    send(array.at[:, columns(device, head)], there, send_sem, recv_sem, device)

                def to_chip(i, carry, act=to_device):
                    each_partner(chips - i, act)
                    return carry

                other_core(to_device)
                lax.fori_loop(1, chips, to_chip, 0)
        return carry

    lax.fori_loop(0, heads, start_head, 0)

    def drain(ref, sem):
        pltpu.make_async_copy(ref, ref, sem).wait()

    def send_res(head, device):
        owned = pl.ds(pl.multiple_of(device * rows, rows), rows)
        for i, array in enumerate((out, out_delta)):
            send(res.at[head, i, owned, :], array.at[:, columns(me, head)], o_send, o_recv.at[i], device)

    def step_chip(i, carry):
        head, step = i // chips, lax.rem(i, chips)
        chip = chip_at(lax.rem(chips - step, chips), -1, 1 - 2 * core)

        @pl.when(step == 0)
        def _():
            drain(kv.at[head], kv_recv.at[head])

        block = pl.ds(pl.multiple_of(chip * pair, pair), pair)
        drain(qs.at[head, block, :], q_recv.at[head, chip])
        primal, tangent = attend(qs[head, block, :], kv[head, 0], kv[head, 1])
        res[head, 0, block, :] = primal
        res[head, 1, block, :] = tangent

        @pl.when(step == 0)
        def _():
            for j, array in enumerate((out, out_delta)):
                pltpu.make_async_copy(
                    res.at[head, j, mine, :], array.at[:, columns(me, head)], o_recv.at[j]
                ).start()
            other_core(functools.partial(send_res, head))

        @pl.when(step != 0)
        def _():
            for turn in range(CORES):
                send_res(head, chip * CORES + lax.rem(core + turn, CORES))

        return carry

    lax.fori_loop(0, heads * chips, step_chip, 0)

    others = pl.ds(0, (n - 1) * rows)
    for head in range(heads):
        drain(kv.at[head, :, others, :], kv_send.at[head])
        drain(qs.at[head, others, :], q_send.at[head])
    drain(res.at[:, :, others, :], o_send)
    drain(out, o_recv.at[0])
    drain(out_delta, o_recv.at[1])


def settle_kernel(a, b, out_a, out_b, sems):
    copies = [pltpu.make_async_copy(a, out_a, sems.at[0]), pltpu.make_async_copy(b, out_b, sems.at[1])]
    for copy in copies:
        copy.start()
    for copy in copies:
        copy.wait()


def settle(a, b, space):
    anywhere = pl.BlockSpec(memory_space=pl.ANY)
    return pl.pallas_call(
        settle_kernel,
        out_shape=(jax.ShapeDtypeStruct(a.shape, a.dtype),) * 2,
        in_specs=[space] * 2,
        out_specs=(anywhere,) * 2,
        scratch_shapes=[pltpu.SemaphoreType.DMA((2,))],
        name="settle",
    )(a, b)


def body(*arrays):
    rows, width = arrays[0].shape
    n = lax.axis_size("ctx")
    tokens = rows * n
    heads = width // HEAD_DIM // n
    anywhere = pl.BlockSpec(memory_space=pl.ANY)
    dma = pltpu.SemaphoreType.DMA
    products = 6 * 2 * tokens * tokens * HEAD_DIM * heads
    result = pl.pallas_call(
        kernel,
        out_shape=(pltpu.VMEM((rows, width), BF16),) * 2,
        in_specs=[anywhere] * 6,
        out_specs=(pl.BlockSpec(memory_space=pltpu.VMEM),) * 2,
        scratch_shapes=[
            pltpu.VMEM((heads, 2, tokens, 2 * HEAD_DIM), BF16),
            pltpu.VMEM((heads, tokens, 2 * HEAD_DIM), BF16),
            pltpu.VMEM((heads, 2, tokens, HEAD_DIM), BF16),
            dma((heads,)), dma((heads,)), dma((heads,)), dma((heads, n // CORES)), dma, dma((2,)),
        ],
        compiler_params=pltpu.CompilerParams(
            collective_id=0, has_side_effects=True, vmem_limit_bytes=60 << 20
        ),
        cost_estimate=pl.CostEstimate(
            flops=products, bytes_accessed=8 * rows * width * 2, transcendentals=tokens * tokens * heads
        ),
        name="attend_exchange",
    )(*arrays)
    result = [pltpu.with_memory_space_constraint(r, pltpu.VMEM) for r in result]
    return settle(*result, pl.BlockSpec(memory_space=pltpu.VMEM))


def solution(mesh):
    spec = P(("dp", "ctx"), None)
    return jax.shard_map(body, mesh=mesh, in_specs=(spec,) * 6, out_specs=(spec,) * 2, check_vma=False)
```

```python
import functools
import math

import jax
import jax.numpy as jnp
from jax import lax
from jax.experimental import pallas as pl
from jax.experimental.pallas import tpu as pltpu
from jax.sharding import PartitionSpec as P

HEAD_DIM = 128
LOG2_E = math.log2(math.e)
MESH = pl.DeviceIdType.MESH
Z = 4
CORES = 2
F32 = jnp.float32
BF16 = jnp.bfloat16


def attend(queries, keys, values):
    factor = HEAD_DIM**-0.5
    across = (((1,), (1,)), ((), ()))
    scores = lax.dot_general(
        queries[:, HEAD_DIM:], keys[:, :HEAD_DIM], across, preferred_element_type=F32
    )
    delta = lax.dot_general(queries, keys, across, preferred_element_type=F32)
    top = jnp.max(scores, axis=1, keepdims=True)
    shifted = jnp.exp2((scores - top) * (factor * LOG2_E))
    scale = 1.0 / jnp.sum(shifted, axis=1, keepdims=True)
    centre = jnp.sum(shifted * delta, axis=1, keepdims=True) * scale
    weights = shifted * scale
    weight_delta = (weights * ((delta - centre) * factor)).astype(BF16)
    both = jnp.dot(weights.astype(BF16), values, preferred_element_type=F32)
    moved = jnp.dot(weight_delta, values[:, :HEAD_DIM], preferred_element_type=F32)
    return both[:, :HEAD_DIM].astype(BF16), (moved + both[:, HEAD_DIM:]).astype(BF16)


def kernel(
    q_in, k_in, v_in, dq_in, dk_in, dv_in,
    out, out_delta,
    kv, qs, res,
    kv_send, kv_recv, q_send, q_recv, o_send, o_recv,
):
    me = lax.axis_index("ctx")
    rows = q_in.shape[0]
    n = lax.axis_size("ctx")
    chips = n // CORES
    y_count = chips // Z
    heads = res.shape[0]
    wide = heads * HEAD_DIM
    pair = CORES * rows
    core = lax.rem(me, CORES)
    z = lax.rem(me // CORES, Z)
    y = me // (CORES * Z)

    def chip_at(step, sign, way):
        dy, dz = step // Z, lax.rem(step, Z)
        there_y = lax.rem(y + sign * dy + y_count, y_count)
        there_z = lax.rem(z + sign * way * dz + Z, Z)
        return there_y * Z + there_z

    def each_partner(step, act):
        chip = chip_at(step, 1, 1 - 2 * core)
        for turn in range(CORES):
            act(chip * CORES + lax.rem(core + turn, CORES))

    def other_core(act):
        for turn in range(1, CORES):
            act(me - core + lax.rem(core + turn, CORES))

    barrier = pltpu.get_barrier_semaphore()

    def greet(device):
        pl.semaphore_signal(barrier, inc=1, device_id={"ctx": device}, device_id_type=MESH)

    for step in range(chips - 1, 0, -1):
        each_partner(step, greet)
    other_core(greet)
    pl.semaphore_wait(barrier, n - 1)

    mine = pl.ds(pl.multiple_of(me * rows, rows), rows)

    def columns(device, head):
        return pl.ds(pl.multiple_of(device * wide + head * HEAD_DIM, HEAD_DIM), HEAD_DIM)

    def send(src, dst, send_sem, recv_sem, device):
        pltpu.make_async_remote_copy(
            src_ref=src, dst_ref=dst, send_sem=send_sem, recv_sem=recv_sem,
            device_id={"ctx": device}, device_id_type=MESH,
        ).start()

    def start_head(head, carry):
        groups = (
            ((k_in, dk_in, v_in, dv_in), (kv.at[head, 0], kv.at[head, 1]), kv_send.at[head], kv_recv.at[head]),
            ((dq_in, q_in), (qs.at[head],), q_send.at[head], q_recv.at[head, me // CORES]),
        )
        for arrays, pairs, send_sem, recv_sem in groups:
            for i, array in enumerate(arrays):
                there = pairs[i // 2].at[mine, pl.ds(i % 2 * HEAD_DIM, HEAD_DIM)]

                def to_device(device, array=array, there=there, send_sem=send_sem, recv_sem=recv_sem):
                    send(array.at[:, columns(device, head)], there, send_sem, recv_sem, device)

                def to_chip(i, carry, act=to_device):
                    each_partner(chips - i, act)
                    return carry

                lax.fori_loop(1, chips, to_chip, 0)
                other_core(to_device)
                pltpu.make_async_copy(array.at[:, columns(me, head)], there, recv_sem).start()
        return carry

    lax.fori_loop(0, heads, start_head, 0)

    def drain(ref, sem):
        pltpu.make_async_copy(ref, ref, sem).wait()

    def send_res(head, device):
        owned = pl.ds(pl.multiple_of(device * rows, rows), rows)
        for i, array in enumerate((out, out_delta)):
            send(res.at[head, i, owned, :], array.at[:, columns(me, head)], o_send, o_recv.at[i], device)

    def step_chip(i, carry):
        head, step = i // chips, lax.rem(i, chips)
        chip = chip_at(lax.rem(chips - step, chips), -1, 1 - 2 * core)

        @pl.when(step == 0)
        def _():
            drain(kv.at[head], kv_recv.at[head])

        block = pl.ds(pl.multiple_of(chip * pair, pair), pair)
        drain(qs.at[head, block, :], q_recv.at[head, chip])
        primal, tangent = attend(qs[head, block, :], kv[head, 0], kv[head, 1])
        res[head, 0, block, :] = primal
        res[head, 1, block, :] = tangent

        @pl.when(step == 0)
        def _():
            for j, array in enumerate((out, out_delta)):
                pltpu.make_async_copy(
                    res.at[head, j, mine, :], array.at[:, columns(me, head)], o_recv.at[j]
                ).start()
            other_core(functools.partial(send_res, head))

        @pl.when(step != 0)
        def _():
            for turn in range(CORES):
                send_res(head, chip * CORES + lax.rem(core + turn, CORES))

        return carry

    lax.fori_loop(0, heads * chips, step_chip, 0)

    others = pl.ds(0, (n - 1) * rows)
    for head in range(heads):
        drain(kv.at[head, :, others, :], kv_send.at[head])
        drain(qs.at[head, others, :], q_send.at[head])
    drain(res.at[:, :, others, :], o_send)
    drain(out, o_recv.at[0])
    drain(out_delta, o_recv.at[1])


def settle_kernel(a, b, out_a, out_b, sems):
    copies = [pltpu.make_async_copy(a, out_a, sems.at[0]), pltpu.make_async_copy(b, out_b, sems.at[1])]
    for copy in copies:
        copy.start()
    for copy in copies:
        copy.wait()


def settle(a, b, space):
    anywhere = pl.BlockSpec(memory_space=pl.ANY)
    return pl.pallas_call(
        settle_kernel,
        out_shape=(jax.ShapeDtypeStruct(a.shape, a.dtype),) * 2,
        in_specs=[space] * 2,
        out_specs=(anywhere,) * 2,
        scratch_shapes=[pltpu.SemaphoreType.DMA((2,))],
        name="settle",
    )(a, b)


def body(*arrays):
    rows, width = arrays[0].shape
    n = lax.axis_size("ctx")
    tokens = rows * n
    heads = width // HEAD_DIM // n
    anywhere = pl.BlockSpec(memory_space=pl.ANY)
    dma = pltpu.SemaphoreType.DMA
    products = 6 * 2 * tokens * tokens * HEAD_DIM * heads
    result = pl.pallas_call(
        kernel,
        out_shape=(pltpu.VMEM((rows, width), BF16),) * 2,
        in_specs=[anywhere] * 6,
        out_specs=(pl.BlockSpec(memory_space=pltpu.VMEM),) * 2,
        scratch_shapes=[
            pltpu.VMEM((heads, 2, tokens, 2 * HEAD_DIM), BF16),
            pltpu.VMEM((heads, tokens, 2 * HEAD_DIM), BF16),
            pltpu.VMEM((heads, 2, tokens, HEAD_DIM), BF16),
            dma((heads,)), dma((heads,)), dma((heads,)), dma((heads, n // CORES)), dma, dma((2,)),
        ],
        compiler_params=pltpu.CompilerParams(
            collective_id=0, has_side_effects=True, vmem_limit_bytes=60 << 20
        ),
        cost_estimate=pl.CostEstimate(
            flops=products, bytes_accessed=8 * rows * width * 2, transcendentals=tokens * tokens * heads
        ),
        name="attend_exchange",
    )(*arrays)
    result = [pltpu.with_memory_space_constraint(r, pltpu.VMEM) for r in result]
    return settle(*result, pl.BlockSpec(memory_space=pltpu.VMEM))


def solution(mesh):
    spec = P(("dp", "ctx"), None)
    return jax.shard_map(body, mesh=mesh, in_specs=(spec,) * 6, out_specs=(spec,) * 2, check_vma=False)
```

```python
import functools
import math

import jax
import jax.numpy as jnp
from jax import lax
from jax.experimental import pallas as pl
from jax.experimental.pallas import tpu as pltpu
from jax.sharding import PartitionSpec as P

HEAD_DIM = 128
LOG2_E = math.log2(math.e)
MESH = pl.DeviceIdType.MESH
Z = 4
CORES = 2
F32 = jnp.float32
BF16 = jnp.bfloat16


def attend(queries, keys, values):
    factor = HEAD_DIM**-0.5
    across = (((1,), (1,)), ((), ()))
    scores = lax.dot_general(
        queries[:, HEAD_DIM:], keys[:, :HEAD_DIM], across, preferred_element_type=F32
    )
    delta = lax.dot_general(queries, keys, across, preferred_element_type=F32)
    top = jnp.max(scores, axis=1, keepdims=True)
    shifted = jnp.exp2((scores - top) * (factor * LOG2_E))
    scale = 1.0 / jnp.sum(shifted, axis=1, keepdims=True)
    centre = jnp.sum(shifted * delta, axis=1, keepdims=True) * scale
    weights = shifted * scale
    weight_delta = (weights * ((delta - centre) * factor)).astype(BF16)
    both = jnp.dot(weights.astype(BF16), values, preferred_element_type=F32)
    moved = jnp.dot(weight_delta, values[:, :HEAD_DIM], preferred_element_type=F32)
    return both[:, :HEAD_DIM].astype(BF16), (moved + both[:, HEAD_DIM:]).astype(BF16)


def kernel(
    q_in, k_in, v_in, dq_in, dk_in, dv_in,
    out,
    kv, qs, res,
    kv_send, kv_recv, q_send, q_recv, o_send, o_recv,
):
    me = lax.axis_index("ctx")
    rows = q_in.shape[0]
    n = lax.axis_size("ctx")
    chips = n // CORES
    y_count = chips // Z
    heads = res.shape[0]
    wide = heads * HEAD_DIM
    pair = CORES * rows
    core = lax.rem(me, CORES)
    z = lax.rem(me // CORES, Z)
    y = me // (CORES * Z)

    def chip_at(step, sign, way):
        dy, dz = step // Z, lax.rem(step, Z)
        there_y = lax.rem(y + sign * dy + y_count, y_count)
        there_z = lax.rem(z + sign * way * dz + Z, Z)
        return there_y * Z + there_z

    def each_partner(step, act):
        chip = chip_at(step, 1, 1 - 2 * core)
        for turn in range(CORES):
            act(chip * CORES + lax.rem(core + turn, CORES))

    def other_core(act):
        for turn in range(1, CORES):
            act(me - core + lax.rem(core + turn, CORES))

    barrier = pltpu.get_barrier_semaphore()

    def greet(device):
        pl.semaphore_signal(barrier, inc=1, device_id={"ctx": device}, device_id_type=MESH)

    for step in range(chips - 1, 0, -1):
        each_partner(step, greet)
    other_core(greet)
    pl.semaphore_wait(barrier, n - 1)

    mine = pl.ds(pl.multiple_of(me * rows, rows), rows)

    def columns(device, head):
        return pl.ds(pl.multiple_of(device * wide + head * HEAD_DIM, HEAD_DIM), HEAD_DIM)

    def send(src, dst, send_sem, recv_sem, device):
        pltpu.make_async_remote_copy(
            src_ref=src, dst_ref=dst, send_sem=send_sem, recv_sem=recv_sem,
            device_id={"ctx": device}, device_id_type=MESH,
        ).start()

    def start_head(head, carry):
        groups = (
            ((k_in, dk_in, v_in, dv_in), (kv.at[head, 0], kv.at[head, 1]), kv_send.at[head], kv_recv.at[head]),
            ((dq_in, q_in), (qs.at[head],), q_send.at[head], q_recv.at[head, me // CORES]),
        )
        for arrays, pairs, send_sem, recv_sem in groups:
            for i, array in enumerate(arrays):
                there = pairs[i // 2].at[mine, pl.ds(i % 2 * HEAD_DIM, HEAD_DIM)]

                def to_device(device, array=array, there=there, send_sem=send_sem, recv_sem=recv_sem):
                    send(array.at[:, columns(device, head)], there, send_sem, recv_sem, device)

                def to_chip(i, carry, act=to_device):
                    each_partner(chips - i, act)
                    return carry

                lax.fori_loop(1, chips, to_chip, 0)
                other_core(to_device)
                pltpu.make_async_copy(array.at[:, columns(me, head)], there, recv_sem).start()
        return carry

    lax.fori_loop(0, heads, start_head, 0)

    def drain(ref, sem):
        pltpu.make_async_copy(ref, ref, sem).wait()

    def send_res(head, device):
        owned = pl.ds(pl.multiple_of(device * rows, rows), rows)
        send(res.at[head, :, owned, :], out.at[:, :, columns(me, head)], o_send, o_recv, device)

    def step_chip(i, carry):
        head, step = i // chips, lax.rem(i, chips)
        chip = chip_at(lax.rem(chips - step, chips), -1, 1 - 2 * core)

        @pl.when(step == 0)
        def _():
            drain(kv.at[head], kv_recv.at[head])

        block = pl.ds(pl.multiple_of(chip * pair, pair), pair)
        drain(qs.at[head, block, :], q_recv.at[head, chip])
        primal, tangent = attend(qs[head, block, :], kv[head, 0], kv[head, 1])
        res[head, 0, block, :] = primal
        res[head, 1, block, :] = tangent

        @pl.when(step == 0)
        def _():
            pltpu.make_async_copy(
                res.at[head, :, mine, :], out.at[:, :, columns(me, head)], o_recv
            ).start()
            other_core(functools.partial(send_res, head))

        @pl.when(step != 0)
        def _():
            for turn in range(CORES):
                send_res(head, chip * CORES + lax.rem(core + turn, CORES))

        return carry

    lax.fori_loop(0, heads * chips, step_chip, 0)

    others = pl.ds(0, (n - 1) * rows)
    for head in range(heads):
        drain(kv.at[head, :, others, :], kv_send.at[head])
        drain(qs.at[head, others, :], q_send.at[head])
    drain(res.at[:, :, others, :], o_send)
    drain(out, o_recv)


def settle_kernel(both, out, out_delta, sems):
    copies = [pltpu.make_async_copy(both.at[i], array, sems.at[i]) for i, array in enumerate((out, out_delta))]
    for copy in copies:
        copy.start()
    for copy in copies:
        copy.wait()


def settle(both):
    anywhere = pl.BlockSpec(memory_space=pl.ANY)
    return pl.pallas_call(
        settle_kernel,
        out_shape=(jax.ShapeDtypeStruct(both.shape[1:], both.dtype),) * 2,
        in_specs=[pl.BlockSpec(memory_space=pltpu.VMEM)],
        out_specs=(anywhere,) * 2,
        scratch_shapes=[pltpu.SemaphoreType.DMA((2,))],
        name="settle",
    )(both)


def body(*arrays):
    rows, width = arrays[0].shape
    n = lax.axis_size("ctx")
    tokens = rows * n
    heads = width // HEAD_DIM // n
    anywhere = pl.BlockSpec(memory_space=pl.ANY)
    dma = pltpu.SemaphoreType.DMA
    products = 6 * 2 * tokens * tokens * HEAD_DIM * heads
    result = pl.pallas_call(
        kernel,
        out_shape=pltpu.VMEM((2, rows, width), BF16),
        in_specs=[anywhere] * 6,
        out_specs=pl.BlockSpec(memory_space=pltpu.VMEM),
        scratch_shapes=[
            pltpu.VMEM((heads, 2, tokens, 2 * HEAD_DIM), BF16),
            pltpu.VMEM((heads, tokens, 2 * HEAD_DIM), BF16),
            pltpu.VMEM((heads, 2, tokens, HEAD_DIM), BF16),
            dma((heads,)), dma((heads,)), dma((heads,)), dma((heads, n // CORES)), dma, dma,
        ],
        compiler_params=pltpu.CompilerParams(
            collective_id=0, has_side_effects=True, vmem_limit_bytes=60 << 20
        ),
        cost_estimate=pl.CostEstimate(
            flops=products, bytes_accessed=8 * rows * width * 2, transcendentals=tokens * tokens * heads
        ),
        name="attend_exchange",
    )(*arrays)
    return settle(pltpu.with_memory_space_constraint(result, pltpu.VMEM))


def solution(mesh):
    spec = P(("dp", "ctx"), None)
    return jax.shard_map(body, mesh=mesh, in_specs=(spec,) * 6, out_specs=(spec,) * 2, check_vma=False)
```

```python
import functools
import math

import jax
import jax.numpy as jnp
from jax import lax
from jax.experimental import pallas as pl
from jax.experimental.pallas import tpu as pltpu
from jax.sharding import PartitionSpec as P

HEAD_DIM = 128
LOG2_E = math.log2(math.e)
MESH = pl.DeviceIdType.MESH
Z = 4
CORES = 2
F32 = jnp.float32
BF16 = jnp.bfloat16


def attend(queries, keys, values):
    factor = HEAD_DIM**-0.5
    across = (((1,), (1,)), ((), ()))
    scores = lax.dot_general(
        queries[:, HEAD_DIM:], keys[:, :HEAD_DIM], across, preferred_element_type=F32
    )
    delta = lax.dot_general(queries, keys, across, preferred_element_type=F32)
    top = jnp.max(scores, axis=1, keepdims=True)
    shifted = jnp.exp2((scores - top) * (factor * LOG2_E))
    scale = 1.0 / jnp.sum(shifted, axis=1, keepdims=True)
    centre = jnp.sum(shifted * delta, axis=1, keepdims=True) * scale
    weights = shifted * scale
    weight_delta = (weights * ((delta - centre) * factor)).astype(BF16)
    both = jnp.dot(weights.astype(BF16), values, preferred_element_type=F32)
    moved = jnp.dot(weight_delta, values[:, :HEAD_DIM], preferred_element_type=F32)
    return both[:, :HEAD_DIM].astype(BF16), (moved + both[:, HEAD_DIM:]).astype(BF16)


def kernel(
    q_in, k_in, v_in, dq_in, dk_in, dv_in,
    out,
    kv, qs, res,
    kv_send, kv_recv, q_send, q_recv, o_send, o_recv,
):
    me = lax.axis_index("ctx")
    rows = q_in.shape[0]
    n = lax.axis_size("ctx")
    chips = n // CORES
    y_count = chips // Z
    heads = res.shape[0]
    wide = heads * HEAD_DIM
    pair = CORES * rows
    core = lax.rem(me, CORES)
    z = lax.rem(me // CORES, Z)
    y = me // (CORES * Z)

    def chip_at(step, sign, way):
        dy, dz = step // Z, lax.rem(step, Z)
        there_y = lax.rem(y + sign * dy + y_count, y_count)
        there_z = lax.rem(z + sign * way * dz + Z, Z)
        return there_y * Z + there_z

    def each_partner(step, act):
        chip = chip_at(step, 1, 1 - 2 * core)
        for turn in range(CORES):
            act(chip * CORES + lax.rem(core + turn, CORES))

    def other_core(act):
        for turn in range(1, CORES):
            act(me - core + lax.rem(core + turn, CORES))

    barrier = pltpu.get_barrier_semaphore()

    def greet(device):
        pl.semaphore_signal(barrier, inc=1, device_id={"ctx": device}, device_id_type=MESH)

    for step in range(chips - 1, 0, -1):
        each_partner(step, greet)
    other_core(greet)
    pl.semaphore_wait(barrier, n - 1)

    mine = pl.ds(pl.multiple_of(me * rows, rows), rows)

    def columns(device, head):
        return pl.ds(pl.multiple_of(device * wide + head * HEAD_DIM, HEAD_DIM), HEAD_DIM)

    def send(src, dst, send_sem, recv_sem, device):
        pltpu.make_async_remote_copy(
            src_ref=src, dst_ref=dst, send_sem=send_sem, recv_sem=recv_sem,
            device_id={"ctx": device}, device_id_type=MESH,
        ).start()

    def start_head(head, carry):
        groups = (
            ((k_in, dk_in, v_in, dv_in), (kv.at[head, 0], kv.at[head, 1]), kv_send.at[head], kv_recv.at[head]),
            ((dq_in, q_in), (qs.at[head],), q_send.at[head], q_recv.at[head, me // CORES]),
        )
        def start(arrays, pairs, send_sem, recv_sem):
            def there(i):
                return pairs[i // 2].at[mine, pl.ds(i % 2 * HEAD_DIM, HEAD_DIM)]

            def to_device(device):
                for i, array in enumerate(arrays):
                    send(array.at[:, columns(device, head)], there(i), send_sem, recv_sem, device)

            def to_chip(i, carry):
                each_partner(chips - i, to_device)
                return carry

            lax.fori_loop(1, chips, to_chip, 0)
            other_core(to_device)
            for i, array in enumerate(arrays):
                pltpu.make_async_copy(array.at[:, columns(me, head)], there(i), recv_sem).start()

        (arrays, pairs, send_sem, recv_sem), queries = groups
        for i in range(0, len(arrays), 2):
            start(arrays[i : i + 2], pairs[i // 2 : i // 2 + 1], send_sem, recv_sem)
        start(*queries)
        return carry

    lax.fori_loop(0, heads, start_head, 0)

    def drain(ref, sem):
        pltpu.make_async_copy(ref, ref, sem).wait()

    def send_res(head, device):
        owned = pl.ds(pl.multiple_of(device * rows, rows), rows)
        send(res.at[head, :, owned, :], out.at[:, :, columns(me, head)], o_send, o_recv, device)

    def step_chip(i, carry):
        head, step = i // chips, lax.rem(i, chips)
        chip = chip_at(lax.rem(chips - step, chips), -1, 1 - 2 * core)

        @pl.when(step == 0)
        def _():
            drain(kv.at[head], kv_recv.at[head])

        block = pl.ds(pl.multiple_of(chip * pair, pair), pair)
        drain(qs.at[head, block, :], q_recv.at[head, chip])
        primal, tangent = attend(qs[head, block, :], kv[head, 0], kv[head, 1])
        res[head, 0, block, :] = primal
        res[head, 1, block, :] = tangent

        @pl.when(step == 0)
        def _():
            pltpu.make_async_copy(
                res.at[head, :, mine, :], out.at[:, :, columns(me, head)], o_recv
            ).start()
            other_core(functools.partial(send_res, head))

        @pl.when(step != 0)
        def _():
            for turn in range(CORES):
                send_res(head, chip * CORES + lax.rem(core + turn, CORES))

        return carry

    lax.fori_loop(0, heads * chips, step_chip, 0)

    others = pl.ds(0, (n - 1) * rows)
    for head in range(heads):
        drain(kv.at[head, :, others, :], kv_send.at[head])
        drain(qs.at[head, others, :], q_send.at[head])
    drain(res.at[:, :, others, :], o_send)
    drain(out, o_recv)


def settle_kernel(both, out, out_delta, sems):
    copies = [pltpu.make_async_copy(both.at[i], array, sems.at[i]) for i, array in enumerate((out, out_delta))]
    for copy in copies:
        copy.start()
    for copy in copies:
        copy.wait()


def settle(both):
    anywhere = pl.BlockSpec(memory_space=pl.ANY)
    return pl.pallas_call(
        settle_kernel,
        out_shape=(jax.ShapeDtypeStruct(both.shape[1:], both.dtype),) * 2,
        in_specs=[pl.BlockSpec(memory_space=pltpu.VMEM)],
        out_specs=(anywhere,) * 2,
        scratch_shapes=[pltpu.SemaphoreType.DMA((2,))],
        name="settle",
    )(both)


def body(*arrays):
    rows, width = arrays[0].shape
    n = lax.axis_size("ctx")
    tokens = rows * n
    heads = width // HEAD_DIM // n
    anywhere = pl.BlockSpec(memory_space=pl.ANY)
    dma = pltpu.SemaphoreType.DMA
    products = 6 * 2 * tokens * tokens * HEAD_DIM * heads
    result = pl.pallas_call(
        kernel,
        out_shape=pltpu.VMEM((2, rows, width), BF16),
        in_specs=[anywhere] * 6,
        out_specs=pl.BlockSpec(memory_space=pltpu.VMEM),
        scratch_shapes=[
            pltpu.VMEM((heads, 2, tokens, 2 * HEAD_DIM), BF16),
            pltpu.VMEM((heads, tokens, 2 * HEAD_DIM), BF16),
            pltpu.VMEM((heads, 2, tokens, HEAD_DIM), BF16),
            dma((heads,)), dma((heads,)), dma((heads,)), dma((heads, n // CORES)), dma, dma,
        ],
        compiler_params=pltpu.CompilerParams(
            collective_id=0, has_side_effects=True, vmem_limit_bytes=60 << 20
        ),
        cost_estimate=pl.CostEstimate(
            flops=products, bytes_accessed=8 * rows * width * 2, transcendentals=tokens * tokens * heads
        ),
        name="attend_exchange",
    )(*arrays)
    return settle(pltpu.with_memory_space_constraint(result, pltpu.VMEM))


def solution(mesh):
    spec = P(("dp", "ctx"), None)
    return jax.shard_map(body, mesh=mesh, in_specs=(spec,) * 6, out_specs=(spec,) * 2, check_vma=False)
```

```python
import functools
import math

import jax
import jax.numpy as jnp
from jax import lax
from jax.experimental import pallas as pl
from jax.experimental.pallas import tpu as pltpu
from jax.sharding import PartitionSpec as P

HEAD_DIM = 128
LOG2_E = math.log2(math.e)
MESH = pl.DeviceIdType.MESH
Z = 4
CORES = 2
F32 = jnp.float32
BF16 = jnp.bfloat16


def attend(queries, keys, values):
    factor = HEAD_DIM**-0.5
    across = (((1,), (1,)), ((), ()))
    scores = lax.dot_general(
        queries[:, HEAD_DIM:], keys[:, :HEAD_DIM], across, preferred_element_type=F32
    )
    delta = lax.dot_general(queries, keys, across, preferred_element_type=F32)
    top = jnp.max(scores, axis=1, keepdims=True)
    shifted = jnp.exp2((scores - top) * (factor * LOG2_E))
    scale = 1.0 / jnp.sum(shifted, axis=1, keepdims=True)
    centre = jnp.sum(shifted * delta, axis=1, keepdims=True) * scale
    weights = shifted * scale
    weight_delta = (weights * ((delta - centre) * factor)).astype(BF16)
    both = jnp.dot(weights.astype(BF16), values, preferred_element_type=F32)
    moved = jnp.dot(weight_delta, values[:, :HEAD_DIM], preferred_element_type=F32)
    return both[:, :HEAD_DIM].astype(BF16), (moved + both[:, HEAD_DIM:]).astype(BF16)


def kernel(
    q_in, k_in, v_in, dq_in, dk_in, dv_in,
    out,
    kv, qs, res,
    kv_send, kv_recv, q_send, q_recv, o_send, o_recv,
):
    me = lax.axis_index("ctx")
    rows = q_in.shape[0]
    n = lax.axis_size("ctx")
    chips = n // CORES
    y_count = chips // Z
    heads = res.shape[0]
    wide = heads * HEAD_DIM
    pair = CORES * rows
    core = lax.rem(me, CORES)
    z = lax.rem(me // CORES, Z)
    y = me // (CORES * Z)

    def chip_at(step, sign, way):
        dy, dz = step // Z, lax.rem(step, Z)
        there_y = lax.rem(y + sign * dy + y_count, y_count)
        there_z = lax.rem(z + sign * way * dz + Z, Z)
        return there_y * Z + there_z

    def each_partner(step, act):
        chip = chip_at(step, 1, 1 - 2 * core)
        for turn in range(CORES):
            act(chip * CORES + lax.rem(core + turn, CORES))

    def other_core(act):
        for turn in range(1, CORES):
            act(me - core + lax.rem(core + turn, CORES))

    barrier = pltpu.get_barrier_semaphore()

    def greet(device):
        pl.semaphore_signal(barrier, inc=1, device_id={"ctx": device}, device_id_type=MESH)

    for step in range(chips - 1, 0, -1):
        each_partner(step, greet)
    other_core(greet)
    pl.semaphore_wait(barrier, n - 1)

    mine = pl.ds(pl.multiple_of(me * rows, rows), rows)

    def columns(device, head):
        return pl.ds(pl.multiple_of(device * wide + head * HEAD_DIM, HEAD_DIM), HEAD_DIM)

    def send(src, dst, send_sem, recv_sem, device):
        pltpu.make_async_remote_copy(
            src_ref=src, dst_ref=dst, send_sem=send_sem, recv_sem=recv_sem,
            device_id={"ctx": device}, device_id_type=MESH,
        ).start()

    def start_head(head, carry):
        groups = (
            ((k_in, dk_in, v_in, dv_in), (kv.at[head, 0], kv.at[head, 1]), kv_send.at[head], kv_recv.at[head]),
            ((dq_in, q_in), (qs.at[head],), q_send.at[head], q_recv.at[head, me // CORES]),
        )
        for arrays, pairs, send_sem, recv_sem in groups:
            for i, array in enumerate(arrays):
                there = pairs[i // 2].at[mine, pl.ds(i % 2 * HEAD_DIM, HEAD_DIM)]

                def to_device(device, array=array, there=there, send_sem=send_sem, recv_sem=recv_sem):
                    send(array.at[:, columns(device, head)], there, send_sem, recv_sem, device)

                def to_chip(i, carry, act=to_device):
                    other_row_last = jnp.where(i == Z, Z, lax.rem(chips + Z - i, chips))
                    each_partner(jnp.where(core == 0, chips - i, other_row_last), act)
                    return carry

                lax.fori_loop(1, chips, to_chip, 0)
                other_core(to_device)
                pltpu.make_async_copy(array.at[:, columns(me, head)], there, recv_sem).start()
        return carry

    lax.fori_loop(0, heads, start_head, 0)

    def drain(ref, sem):
        pltpu.make_async_copy(ref, ref, sem).wait()

    def send_res(head, device):
        owned = pl.ds(pl.multiple_of(device * rows, rows), rows)
        send(res.at[head, :, owned, :], out.at[:, :, columns(me, head)], o_send, o_recv, device)

    def step_chip(i, carry):
        head, step = i // chips, lax.rem(i, chips)
        chip = chip_at(lax.rem(chips - step, chips), -1, 1 - 2 * core)

        @pl.when(step == 0)
        def _():
            drain(kv.at[head], kv_recv.at[head])

        block = pl.ds(pl.multiple_of(chip * pair, pair), pair)
        drain(qs.at[head, block, :], q_recv.at[head, chip])
        primal, tangent = attend(qs[head, block, :], kv[head, 0], kv[head, 1])
        res[head, 0, block, :] = primal
        res[head, 1, block, :] = tangent

        @pl.when(step == 0)
        def _():
            pltpu.make_async_copy(
                res.at[head, :, mine, :], out.at[:, :, columns(me, head)], o_recv
            ).start()
            other_core(functools.partial(send_res, head))

        @pl.when(step != 0)
        def _():
            for turn in range(CORES):
                send_res(head, chip * CORES + lax.rem(core + turn, CORES))

        return carry

    lax.fori_loop(0, heads * chips, step_chip, 0)

    others = pl.ds(0, (n - 1) * rows)
    for head in range(heads):
        drain(kv.at[head, :, others, :], kv_send.at[head])
        drain(qs.at[head, others, :], q_send.at[head])
    drain(res.at[:, :, others, :], o_send)
    drain(out, o_recv)


def settle_kernel(both, out, out_delta, sems):
    copies = [pltpu.make_async_copy(both.at[i], array, sems.at[i]) for i, array in enumerate((out, out_delta))]
    for copy in copies:
        copy.start()
    for copy in copies:
        copy.wait()


def settle(both):
    anywhere = pl.BlockSpec(memory_space=pl.ANY)
    return pl.pallas_call(
        settle_kernel,
        out_shape=(jax.ShapeDtypeStruct(both.shape[1:], both.dtype),) * 2,
        in_specs=[pl.BlockSpec(memory_space=pltpu.VMEM)],
        out_specs=(anywhere,) * 2,
        scratch_shapes=[pltpu.SemaphoreType.DMA((2,))],
        name="settle",
    )(both)


def body(*arrays):
    rows, width = arrays[0].shape
    n = lax.axis_size("ctx")
    tokens = rows * n
    heads = width // HEAD_DIM // n
    anywhere = pl.BlockSpec(memory_space=pl.ANY)
    dma = pltpu.SemaphoreType.DMA
    products = 6 * 2 * tokens * tokens * HEAD_DIM * heads
    result = pl.pallas_call(
        kernel,
        out_shape=pltpu.VMEM((2, rows, width), BF16),
        in_specs=[anywhere] * 6,
        out_specs=pl.BlockSpec(memory_space=pltpu.VMEM),
        scratch_shapes=[
            pltpu.VMEM((heads, 2, tokens, 2 * HEAD_DIM), BF16),
            pltpu.VMEM((heads, tokens, 2 * HEAD_DIM), BF16),
            pltpu.VMEM((heads, 2, tokens, HEAD_DIM), BF16),
            dma((heads,)), dma((heads,)), dma((heads,)), dma((heads, n // CORES)), dma, dma,
        ],
        compiler_params=pltpu.CompilerParams(
            collective_id=0, has_side_effects=True, vmem_limit_bytes=60 << 20
        ),
        cost_estimate=pl.CostEstimate(
            flops=products, bytes_accessed=8 * rows * width * 2, transcendentals=tokens * tokens * heads
        ),
        name="attend_exchange",
    )(*arrays)
    return settle(pltpu.with_memory_space_constraint(result, pltpu.VMEM))


def solution(mesh):
    spec = P(("dp", "ctx"), None)
    return jax.shard_map(body, mesh=mesh, in_specs=(spec,) * 6, out_specs=(spec,) * 2, check_vma=False)
```
